256 devices in a mesh: seg: 16 (over y, x), sec: 16 (over z, core).
Axes of the slice: x: 4, y: 4, z: 8, core: 2. Of those that a mesh axis runs over, the one named last changes fastest.
Arguments:
- left_env: bfloat16 [16, 400, 256, 256], P('seg', 'sec'), as said below
- right_env: bfloat16 [16, 400, 256, 256], P('seg', 'sec'), as said below
- edge_site: bfloat16 [16, 256, 256], P('seg'), may hold values from -0.375 to 0.375
- psi_one: bfloat16 [16, 256, 256], P('seg'), may hold values from -6 to 6
- psi_two: bfloat16 [16, 256, 256], P('seg'), may hold values from -6 to 6
- mpo_gain: float32 [16, 400], P('seg', 'sec'), may hold values from 0.5 to 2
- kept: int32 [16, 2], P('seg'), may hold values from 64 to 256, as said below
Outputs:
- psi_first: float32 [16, 256, 256], P('seg', 'sec')
- psi_second: float32 [16, 256, 256], P('seg', 'sec')
The draws below stay inside these ranges and needn't reach their ends.
Inputs may be any that keep to these rules, and one draw needn't show every extreme that they name: `kept`: some entry equals 256 and some equals 64. `left_env`: every [256, 256] block is symmetric, with entries of order (26214400) ** -0.25. `right_env`: every [256, 256] block is symmetric, with entries of order (26214400) ** -0.25.
All inputs are finite; a program needn't handle non-finite values.
Results may differ from the reference program's by a relative error of at most 0.03.
Values may be sent and summed in bfloat16 or wider, within the bound.
No kernel may reach another device: no remote copies, remote signals or barrier semaphores. Data moves between devices by JAX's collectives and lax.ppermute only.
A program may use at most 64 MiB of HBM per device.

```python
import math
import jax
import jax.numpy as jnp
from jax import lax

M = 256
W = 400
ITERS = 3
SEGS = 16


def symmetrize(raw_draw, spread):
    return (raw_draw + jnp.swapaxes(raw_draw, -1, -2)) * (spread * 0.7071067811865476)


def draw_left_env(key, part):
    key = jax.random.fold_in(key, 11)
    array_shape = (SEGS, W, M, M)
    raw_draw = jax.random.normal(key, array_shape, jnp.float32)
    return symmetrize(raw_draw, (W * M * M) ** (-0.25)).astype(jnp.bfloat16)


def draw_right_env(key, part):
    key = jax.random.fold_in(key, 12)
    array_shape = (SEGS, W, M, M)
    raw_draw = jax.random.normal(key, array_shape, jnp.float32)
    return symmetrize(raw_draw, (W * M * M) ** (-0.25)).astype(jnp.bfloat16)


def draw_kept(key, part):
    key = jax.random.fold_in(key, 13)
    live_rows = jax.random.randint(key, (SEGS, 2), M // 4, M + 1, dtype=jnp.int32)
    live_rows = live_rows.at[0, 0].set(M)
    return live_rows.at[1, 1].set(M // 4)


def block_scale(key, shape, shards, smallest, top_value):
    def one(dim, blocks):
        draws = jax.random.uniform(jax.random.fold_in(jax.random.fold_in(key, 6), dim), (blocks,), jnp.float32, smallest / len(shards), top_value / len(shards))
        return jnp.repeat(jnp.exp(draws), shape[dim] // blocks).reshape((-1,) + (1,) * (len(shape) - dim - 1))

    factor_of = one(*shards[0])
    for cut in shards[1:]:
        factor_of = factor_of * one(*cut)
    return factor_of


def noise(key, dims, width, limit, shards=(), kind=jnp.bfloat16):
    factor_of = block_scale(key, dims, shards, -0.22, 0.18) if shards else 1.0
    result = jax.random.normal(key, dims, jnp.float32) * width * factor_of
    return jnp.minimum(jnp.maximum(result, -limit), limit).astype(kind)


def setup_inputs(seed: int = 0) -> dict:
    key_of = jax.random.split(jax.random.key(seed), 8)
    return {
        "left_env": draw_left_env(jax.random.fold_in(key_of[7], 71), 0),
        "right_env": draw_right_env(jax.random.fold_in(key_of[7], 71), 0),
        "edge_site": noise(key_of[2], (SEGS, M, M), M ** -0.5, 0.375, ((0, 16),)),
        "psi_one": noise(key_of[3], (SEGS, M, M), 1.0, 6.0, ((0, 16),)),
        "psi_two": noise(key_of[4], (SEGS, M, M), 1.0, 6.0, ((0, 16),)),
        "mpo_gain": jnp.clip(jnp.exp(math.log(2.0) - 1.3862944 * jax.random.uniform(key_of[5], (SEGS, W), jnp.float32) ** block_scale(key_of[5], (SEGS, W), ((0, 16), (1, 16)), -0.2, 0.2)), 0.5, 2.0),
        "kept": draw_kept(jax.random.fold_in(key_of[7], 71), 0),
    }


epsilon = 1e-06
descent = 0.3

def apply_block(left_block, right_block, vector_bf):
    mpo_terms = left_block.shape[0]
    states = left_block.shape[1]
    partial_prod = jnp.dot(left_block.reshape(mpo_terms * states, states), vector_bf, preferred_element_type=jnp.float32)
    partial_prod = partial_prod.astype(jnp.bfloat16).reshape(mpo_terms, states, states)
    return jnp.einsum('wil,wjl->ij', partial_prod.astype(jnp.float32), right_block.astype(jnp.float32))

def rescale(vector, norm_sq):
    return M * vector / jnp.sqrt(norm_sq + epsilon)

def relax_block(left_block, right_block, start, live):
    live_mask = (jnp.arange(M) < live).astype(jnp.float32)[:, None]
    initial = start.astype(jnp.float32) * live_mask
    vector = rescale(initial, jnp.sum(initial * initial))
    for sweep_step in range(ITERS):
        product = apply_block(left_block, right_block, vector.astype(jnp.bfloat16)) * live_mask
        energy = jnp.sum(vector * product) / jnp.sum(vector * vector)
        stepped = vector - descent * (product - energy * vector)
        vector = rescale(stepped, jnp.sum(stepped * stepped))
    return vector

def build_outgoing(args):
    left_block, site_tensor, gain_row = args
    mpo_terms = left_block.shape[0]
    halfway = jnp.dot(left_block.reshape(mpo_terms * M, M), site_tensor, preferred_element_type=jnp.float32)
    halfway = halfway.astype(jnp.bfloat16).reshape(mpo_terms, M, M)
    outgoing = jnp.einsum('ki,wkj->wij', site_tensor.astype(jnp.float32), halfway.astype(jnp.float32))
    return (outgoing * gain_row[:, None, None]).astype(jnp.bfloat16)

def per_segment(args):
    left_block, right_block, incoming, start_one, start_two, gain_row, live_pair = args
    first = relax_block(left_block, right_block, start_one, live_pair[0])
    site_left = (first * M ** (-0.5)).astype(jnp.bfloat16)
    mpo_terms = right_block.shape[0]
    halfway = jnp.dot(right_block.reshape(mpo_terms * M, M), site_left.T, preferred_element_type=jnp.float32)
    halfway = halfway.astype(jnp.bfloat16).reshape(mpo_terms, M, M)
    right_next = jnp.einsum('ik,wkj->wij', site_left.astype(jnp.float32), halfway.astype(jnp.float32))
    right_next = (right_next * gain_row[:, None, None]).astype(jnp.bfloat16)
    second = relax_block(incoming, right_next, start_two, live_pair[1])
    return (first, second)

def reference(left_env, right_env, edge_site, psi_one, psi_two, mpo_gain, kept):
    outgoing = lax.map(build_outgoing, (left_env, edge_site, mpo_gain))
    incoming = jnp.concatenate([left_env[:1], outgoing[:-1]], axis=0)
    first, second = lax.map(per_segment, (left_env, right_env, incoming, psi_one, psi_two, mpo_gain, kept))
    return (first, second)
```

```python
import functools

import jax
import jax.numpy as jnp
from jax import lax
from jax.experimental import pallas as pl
from jax.experimental.pallas import tpu as pltpu
from jax.sharding import PartitionSpec as P

ITERS = 3
EPSILON = 1e-06
DESCENT = 0.3
CHUNK = 5
VMEM_LIMIT = 40 * 1024 * 1024

F32 = jnp.float32
BF16 = jnp.bfloat16


def dot(a, b, dims=((1,), (0,))):
    return lax.dot_general(a, b, (dims, ((), ())), preferred_element_type=F32)


def live_rows(shape, live):
    return lax.broadcasted_iota(jnp.int32, shape, 0) < live


def normalised(z, states):
    return z * (states / jnp.sqrt(jnp.sum(z * z) + EPSILON))


def stepped(vector, product, states):
    energy = jnp.sum(vector * product) / jnp.sum(vector * vector)
    return normalised(vector - DESCENT * (product - energy * vector), states)


def block_copies(left, right, left_buf, right_buf, sems):
    terms = left_buf.shape[0]
    chunk = CHUNK if terms % CHUNK == 0 else 1
    return chunk, [
        (
            pltpu.make_async_copy(left.at[0, pl.ds(n, chunk)], left_buf.at[pl.ds(n, chunk)], sems.at[0, n // chunk]),
            pltpu.make_async_copy(right.at[0, pl.ds(n, chunk)], right_buf.at[pl.ds(n, chunk)], sems.at[1, n // chunk]),
        )
        for n in range(0, terms, chunk)
    ]


def contract(vector, copies, chunk, left_buf, right_buf, acc, weight=None):
    states = vector.shape[0]
    for index, (left_copy, right_copy) in enumerate(copies):
        left_copy.wait()
        right_copy.wait()
        first = index * chunk
        terms = dot(left_buf[first : first + chunk].reshape(chunk * states, states), vector)
        total = None
        for n in range(chunk):
            term = terms[n * states : (n + 1) * states]
            if weight is not None:
                term = term * weight(first + n)
            part = dot(term.astype(BF16), right_buf[first + n])
            total = part if total is None else total + part
        if index == 0:
            acc[...] = total
        else:
            acc[...] += total


def hand_out(acc, mine, theirs):
    half = mine.shape[0]
    core = lax.rem(lax.axis_index("sec"), 2)
    mine[...] = acc[pl.ds(pl.multiple_of(core * half, half), half), :].astype(BF16)
    theirs[...] = acc[pl.ds(pl.multiple_of((1 - core) * half, half), half), :].astype(BF16)


def product_of(summed, live):
    states = summed.shape[2]
    product = summed[...].reshape(states, states).astype(F32)
    return jnp.where(live_rows(product.shape, live), product, 0.0)


def first_start(kept, start, left, right, vector, mine, theirs, left_buf, right_buf, acc, sems):
    chunk, copies = block_copies(left, right, left_buf, right_buf, sems)
    for pair in copies:
        pair[0].start()
        pair[1].start()
    states = start.shape[1]
    begun = jnp.where(live_rows((states, states), kept[0, 0]), start[0].astype(F32), 0.0)
    current = normalised(begun, states)
    vector[...] = current
    contract(current.astype(BF16), copies, chunk, left_buf, right_buf, acc)
    hand_out(acc, mine, theirs)


def first_step(kept, vector, summed, left, right, after, mine, theirs, left_buf, right_buf, acc, sems):
    chunk, copies = block_copies(left, right, left_buf, right_buf, sems)
    for pair in copies:
        pair[0].start()
        pair[1].start()
    states = vector.shape[1]
    current = stepped(vector[...], product_of(summed, kept[0, 0]), states)
    after[...] = current
    contract(current.astype(BF16), copies, chunk, left_buf, right_buf, acc)
    hand_out(acc, mine, theirs)


def second_blocks(left, arrived, right, left_buf, right_buf, sems):
    chunk, copies = block_copies(arrived, right, left_buf, right_buf, sems)
    at_start = lax.axis_index("seg") == 0

    @pl.when(at_start)
    def _():
        for index in range(len(copies)):
            part = pl.ds(index * chunk, chunk)
            pltpu.make_async_copy(left.at[0, part], left_buf.at[part], sems.at[0, index]).start()

    @pl.when(jnp.logical_not(at_start))
    def _():
        for left_copy, _ in copies:
            left_copy.start()

    for _, right_copy in copies:
        right_copy.start()
    return chunk, copies, at_start


def second_apply(current, site, edge, gain, gain_before, blocks, left_buf, right_buf, acc, mine, theirs):
    chunk, copies, at_start = blocks
    shape = edge.shape
    one = lax.broadcasted_iota(jnp.int32, shape, 0) == lax.broadcasted_iota(jnp.int32, shape, 1)
    edge = jnp.where(at_start, one.astype(F32), edge.astype(F32)).astype(BF16)
    inner = dot(current.astype(BF16), site).astype(BF16)
    inner = dot(edge, inner).astype(BF16)

    def weight(n):
        return gain[0, n] * jnp.where(at_start, 1.0, gain_before[0, n])

    contract(inner, copies, chunk, left_buf, right_buf, acc, weight)
    outer = dot(acc[...].astype(BF16), site, ((1,), (1,))).astype(BF16)
    acc[...] = dot(edge, outer, ((0,), (0,)))
    hand_out(acc, mine, theirs)


def second_start(
    kept, vector, summed, start, edge, gain, gain_before, left, arrived, right,
    rows, site, after, mine, theirs, left_buf, right_buf, acc, sems,
):
    blocks = second_blocks(left, arrived, right, left_buf, right_buf, sems)
    states = vector.shape[1]
    share = rows.shape[1]
    acc[...] = stepped(vector[...], product_of(summed, kept[0, 0]), states)
    rows[0] = acc[pl.ds(pl.multiple_of(lax.axis_index("sec") * share, share), share), :]
    site_left = (acc[...] * states**-0.5).astype(BF16)
    site[...] = site_left
    begun = jnp.where(live_rows((states, states), kept[0, 1]), start[0].astype(F32), 0.0)
    current = normalised(begun, states)
    after[...] = current
    second_apply(current, site_left, edge[0], gain, gain_before, blocks, left_buf, right_buf, acc, mine, theirs)


def second_step(
    kept, vector, summed, site, edge, gain, gain_before, left, arrived, right,
    after, mine, theirs, left_buf, right_buf, acc, sems,
):
    blocks = second_blocks(left, arrived, right, left_buf, right_buf, sems)
    states = vector.shape[1]
    current = stepped(vector[...], product_of(summed, kept[0, 1]), states)
    after[...] = current
    second_apply(current, site[...], edge[0], gain, gain_before, blocks, left_buf, right_buf, acc, mine, theirs)


def second_end(kept, vector, summed, rows, whole):
    states = vector.shape[1]
    share = rows.shape[1]
    whole[...] = stepped(vector[...], product_of(summed, kept[0, 1]), states)
    rows[0] = whole[pl.ds(pl.multiple_of(lax.axis_index("sec") * share, share), share), :]


def on_device(left_env, right_env, edge_site, psi_one, psi_two, mpo_gain, kept):
    terms, states = left_env.shape[1], left_env.shape[2]
    sections, segments = lax.axis_size("sec"), lax.axis_size("seg")
    chips, half, share = sections // 2, states // 2, states // sections
    pairs = [[2 * n, 2 * n + 1] for n in range(chips)]
    columns = [[2 * n + core for n in range(chips)] for core in range(2)]
    onward = [(n, n + 1) for n in range(segments - 1)]

    smem = pl.BlockSpec(memory_space=pltpu.SMEM)
    vmem = pl.BlockSpec(memory_space=pltpu.VMEM)
    hbm = pl.BlockSpec(memory_space=pl.ANY)
    block = jax.ShapeDtypeStruct((states, states), F32)
    site_block = jax.ShapeDtypeStruct((states, states), BF16)
    half_block = jax.ShapeDtypeStruct((half, states), BF16)
    rows_block = jax.ShapeDtypeStruct((1, share, states), F32)
    buffers = [
        pltpu.VMEM((terms, states, states), BF16),
        pltpu.VMEM((terms, states, states), BF16),
        pltpu.VMEM((states, states), F32),
        pltpu.SemaphoreType.DMA((2, terms // CHUNK if terms % CHUNK == 0 else terms)),
    ]
    params = pltpu.CompilerParams(vmem_limit_bytes=VMEM_LIMIT)
    cost = pl.CostEstimate(
        flops=4 * terms * states**3, bytes_accessed=4 * terms * states**2, transcendentals=0
    )

    def call(kernel, ins, outs, name, scratch=buffers, cost=cost):
        return pl.pallas_call(
            kernel,
            in_specs=ins,
            out_specs=[vmem] * len(outs),
            out_shape=outs,
            scratch_shapes=scratch,
            compiler_params=params,
            cost_estimate=cost,
            name=name,
        )

    def summed(mine, theirs):
        other = lax.ppermute(theirs, "sec", [(n, n ^ 1) for n in range(sections)])
        chip = (mine.astype(F32) + other.astype(F32)).astype(BF16)
        spread = jnp.broadcast_to(chip[None], (chips, half, states))
        parts = lax.all_to_all(spread, "sec", 0, 0, axis_index_groups=columns)
        total = jnp.sum(parts.astype(F32), axis=0).astype(BF16)
        return lax.all_gather(total, "sec", axis=0, axis_index_groups=pairs)

    arrived = lax.ppermute(left_env, "seg", onward)
    edge = lax.ppermute(edge_site, "seg", onward)
    gain_before = lax.ppermute(mpo_gain, "seg", onward)

    vector, mine, theirs = call(
        first_start, [smem, vmem, hbm, hbm], [block, half_block, half_block], "first_start"
    )(kept, psi_one, left_env, right_env)
    for _ in range(ITERS - 1):
        vector, mine, theirs = call(
            first_step, [smem, vmem, vmem, hbm, hbm], [block, half_block, half_block], "first_step"
        )(kept, vector, summed(mine, theirs), left_env, right_env)

    first_rows, site, vector, mine, theirs = call(
        second_start,
        [smem, vmem, vmem, vmem, vmem, smem, smem, hbm, hbm, hbm],
        [rows_block, site_block, block, half_block, half_block],
        "second_start",
    )(kept, vector, summed(mine, theirs), psi_two, edge, mpo_gain, gain_before, left_env, arrived, right_env)
    for _ in range(ITERS - 1):
        vector, mine, theirs = call(
            second_step,
            [smem, vmem, vmem, vmem, vmem, smem, smem, hbm, hbm, hbm],
            [block, half_block, half_block],
            "second_step",
        )(kept, vector, summed(mine, theirs), site, edge, mpo_gain, gain_before, left_env, arrived, right_env)
    (second_rows,) = call(
        second_end,
        [smem, vmem, vmem],
        [rows_block],
        "second_end",
        [pltpu.VMEM((states, states), F32)],
        None,
    )(kept, vector, summed(mine, theirs))
    return first_rows, second_rows


def solution(mesh):
    placed = (
        P("seg", "sec", None, None),
        P("seg", "sec", None, None),
        P("seg", None, None),
        P("seg", None, None),
        P("seg", None, None),
        P("seg", "sec"),
        P("seg", None),
    )
    return jax.shard_map(
        on_device,
        mesh=mesh,
        in_specs=placed,
        out_specs=(P("seg", "sec", None), P("seg", "sec", None)),
        check_vma=False,
    )
```

```python
import jax
import jax.numpy as jnp
from jax import lax
from jax.experimental import pallas as pl
from jax.experimental.pallas import tpu as pltpu
from jax.sharding import PartitionSpec as P

ITERS = 3
EPSILON = 1e-06
DESCENT = 0.3
CHUNK = 5
MIB = 1024 * 1024

F32 = jnp.float32
BF16 = jnp.bfloat16


def dot(a, b, dims=((1,), (0,))):
    return lax.dot_general(a, b, (dims, ((), ())), preferred_element_type=F32)


def live_rows(shape, live):
    return lax.broadcasted_iota(jnp.int32, shape, 0) < live


def begun(start, live):
    states = start.shape[-1]
    block = start[...].reshape(states, states).astype(F32)
    block = jnp.where(live_rows(block.shape, live), block, 0.0)
    return block * (states / jnp.sqrt(jnp.sum(block * block) + EPSILON))


def stepped(vector, mine, other, live):
    states = vector.shape[-1]
    low = lax.rem(lax.axis_index("sec"), 2) == 0
    own, far = mine[...].astype(F32), other[...].astype(F32)
    product = jnp.concatenate([jnp.where(low, own, far), jnp.where(low, far, own)], axis=0)
    product = jnp.where(live_rows(product.shape, live), product, 0.0)
    current = vector[...]
    xx, xy = jnp.sum(current * current), jnp.sum(current * product)
    yy = jnp.sum(product * product)
    energy = xy / xx
    norm = xx + DESCENT * DESCENT * jnp.maximum(yy - energy * xy, 0.0)
    scale = states / jnp.sqrt(norm + EPSILON)
    return current * (scale * (1.0 + DESCENT * energy)) - product * (scale * DESCENT)


def own_rows(block, rows):
    share = rows.shape[1]
    rows[0] = block[pl.ds(pl.multiple_of(lax.axis_index("sec") * share, share), share), :]


def chunk_of(terms):
    return CHUNK if terms % CHUNK == 0 else 1


def contract(vector, left, right, acc, landed=None):
    states = vector.shape[0]
    terms = left.shape[0]
    chunk = chunk_of(terms)
    for first in range(0, terms, chunk):
        if landed is not None:
            landed(first // chunk)
        inner = dot(left[first : first + chunk].reshape(chunk * states, states), vector)
        total = None
        for n in range(chunk):
            part = dot(inner[n * states : (n + 1) * states].astype(BF16), right[first + n])
            total = part if total is None else total + part
        if first == 0:
            acc[...] = total
        else:
            acc[...] += total


def hand_out(acc, mine, theirs):
    half = mine.shape[0]
    core = lax.rem(lax.axis_index("sec"), 2)
    mine[...] = acc[pl.ds(pl.multiple_of(core * half, half), half), :].astype(BF16)
    theirs[...] = acc[pl.ds(pl.multiple_of((1 - core) * half, half), half), :].astype(BF16)


def first_start(kept, start, left, right, vector, mine, theirs, left_buf, right_buf, acc, sems):
    terms = left_buf.shape[0]
    chunk = chunk_of(terms)
    copies = []
    for index in range(terms // chunk):
        part = pl.ds(index * chunk, chunk)
        copies.append(
            (
                pltpu.make_async_copy(left.at[0, part], left_buf.at[part], sems.at[0, index]),
                pltpu.make_async_copy(right.at[0, part], right_buf.at[part], sems.at[1, index]),
            )
        )
    for left_copy, right_copy in copies:
        left_copy.start()
        right_copy.start()

    def landed(index):
        copies[index][0].wait()
        copies[index][1].wait()

    current = begun(start, kept[0, 0])
    vector[...] = current
    contract(current.astype(BF16), left_buf, right_buf, acc, landed)
    hand_out(acc, mine, theirs)


def first_step(kept, vector, summed, other, left, right, after, mine, theirs, acc):
    current = stepped(vector, summed, other, kept[0, 0])
    after[...] = current
    contract(current.astype(BF16), left.at[0], right.at[0], acc)
    hand_out(acc, mine, theirs)


def place(shape):
    return lax.broadcasted_iota(jnp.int32, shape, 0), lax.broadcasted_iota(jnp.int32, shape, 1)


def pack(gain, left, edge, package):
    terms, states = left.shape[1], left.shape[2]
    row, column = place((states, states))
    pairs = terms // 2

    def scaled(n):
        return left[0, n].astype(F32) * gain[0, n]

    for n in range(pairs):
        second = scaled(2 * n + 1)
        slab = jnp.where(row >= column, scaled(2 * n), second)
        package[n * states : (n + 1) * states] = slab.astype(BF16)
        diagonal = jnp.sum(jnp.where(row == column, second, 0.0), axis=0, keepdims=True)
        base = (pairs + terms % 2 + 1) * states + 16 * n
        package[base : base + 16] = jnp.broadcast_to(diagonal, (16, states)).astype(BF16)
    if terms % 2:
        package[pairs * states : (pairs + 1) * states] = scaled(terms - 1).astype(BF16)
    last = pairs + terms % 2
    package[last * states : (last + 1) * states] = edge[0]


def unpack(kept, gain, left, package, start, incoming, site, vector, turned):
    terms, states = left.shape[1], left.shape[2]
    row, column = place((states, states))
    pairs = terms // 2
    at_start = lax.axis_index("seg") == 0

    @pl.when(at_start)
    def _():
        for n in range(terms):
            incoming[n] = (left[0, n].astype(F32) * gain[0, n]).astype(BF16)
        site[...] = jnp.where(row == column, 1.0, 0.0).astype(BF16)

    @pl.when(jnp.logical_not(at_start))
    def _():
        for n in range(pairs):
            slab = package[n * states : (n + 1) * states].astype(F32)
            mirrored = slab.T
            base = (pairs + terms % 2 + 1) * states + 16 * n
            diagonal = package[base : base + 16].astype(F32)[0:1]
            one = jnp.where(row >= column, slab, mirrored)
            two = jnp.where(row < column, slab, jnp.where(row == column, diagonal, mirrored))
            incoming[2 * n] = (one * gain[0, 2 * n]).astype(BF16)
            incoming[2 * n + 1] = (two * gain[0, 2 * n + 1]).astype(BF16)
        if terms % 2:
            slab = package[pairs * states : (pairs + 1) * states].astype(F32)
            incoming[terms - 1] = (slab * gain[0, terms - 1]).astype(BF16)
        last = pairs + terms % 2
        site[...] = package[last * states : (last + 1) * states]

    current = begun(start, kept[0, 1])
    vector[...] = current
    turned[...] = dot(site[...], current.astype(BF16)).astype(BF16)


def second_apply(inner, edge, site, incoming, right, acc, mine, theirs):
    contract(inner, incoming, right.at[0], acc)
    outer = dot(acc[...].astype(BF16), site, ((1,), (1,))).astype(BF16)
    acc[...] = dot(edge[...], outer, ((0,), (0,)))
    hand_out(acc, mine, theirs)


def second_start(
    kept, vector, summed, other, turned, edge, incoming, right, rows, site, mine, theirs, acc
):
    states = vector.shape[1]
    acc[...] = stepped(vector, summed, other, kept[0, 0])
    own_rows(acc, rows)
    site_left = (acc[...] * states**-0.5).astype(BF16)
    site[...] = site_left
    inner = dot(turned[...], site_left).astype(BF16)
    second_apply(inner, edge, site_left, incoming, right, acc, mine, theirs)


def second_step(
    kept, vector, summed, other, site, edge, incoming, right, after, mine, theirs, acc
):
    current = stepped(vector, summed, other, kept[0, 1])
    after[...] = current
    inner = dot(current.astype(BF16), site[...]).astype(BF16)
    inner = dot(edge[...], inner).astype(BF16)
    second_apply(inner, edge, site[...], incoming, right, acc, mine, theirs)


def second_end(kept, vector, summed, other, rows, acc):
    acc[...] = stepped(vector, summed, other, kept[0, 1])
    own_rows(acc, rows)


def add(*refs):
    total = refs[0][...].astype(F32)
    for ref in refs[1:-1]:
        total = total + ref[...].astype(F32)
    refs[-1][...] = total.astype(BF16)


def on_device(left_env, right_env, edge_site, psi_one, psi_two, mpo_gain, kept):
    terms, states = left_env.shape[1], left_env.shape[2]
    sections, segments = lax.axis_size("sec"), lax.axis_size("seg")
    share, half = states // sections, states // 2

    smem = pl.BlockSpec(memory_space=pltpu.SMEM)
    vmem = pl.BlockSpec(memory_space=pltpu.VMEM)
    hbm = pl.BlockSpec(memory_space=pl.ANY)

    def shape(*dims, dtype=BF16):
        return jax.ShapeDtypeStruct(dims, dtype)

    block = shape(states, states, dtype=F32)
    halves = [shape(half, states)] * 2
    rows = shape(1, share, states, dtype=F32)
    acc = pltpu.VMEM((states, states), F32)
    apply_cost = pl.CostEstimate(
        flops=4 * terms * states**3, bytes_accessed=4 * terms * states**2, transcendentals=0
    )

    def call(kernel, ins, outs, scratch=(acc,), limit=12 * MIB, cost=None):
        return pl.pallas_call(
            kernel,
            in_specs=ins,
            out_specs=[vmem] * len(outs),
            out_shape=outs,
            scratch_shapes=list(scratch),
            compiler_params=pltpu.CompilerParams(vmem_limit_bytes=limit),
            cost_estimate=cost,
            name=kernel.__name__,
        )

    def moved(value, target):
        return lax.ppermute(value, "sec", [(n, target(n) % sections) for n in range(sections)])

    def added(*values):
        return call(add, [vmem] * len(values), halves[:1], (), 2 * MIB)(*values)[0]

    def summed(mine, theirs):
        total = added(mine, moved(theirs, lambda n: n ^ 1))
        total = added(total, moved(total, lambda n: n ^ 2))
        parts = [moved(total, lambda n, step=step: n + step) for step in range(4, sections, 4)]
        total = added(total, *parts)
        return total, moved(total, lambda n: n ^ 1)

    chunks = terms // chunk_of(terms)
    buffer = pltpu.VMEM((terms, states, states), BF16)
    vector, mine, theirs = call(
        first_start,
        [smem, vmem, hbm, hbm],
        [block, *halves],
        [buffer, buffer, acc, pltpu.SemaphoreType.DMA((2, chunks))],
        61 * MIB,
        apply_cost,
    )(kept, psi_one, left_env, right_env)

    slabs = terms // 2 + terms % 2 + 1
    (package,) = call(
        pack, [smem, vmem, vmem], [shape(slabs * states + 16 * (terms // 2), states)], ()
    )(mpo_gain, left_env, edge_site)
    package = lax.ppermute(package, "seg", [(n, n + 1) for n in range(segments - 1)])

    for _ in range(ITERS - 1):
        vector, mine, theirs = call(
            first_step, [smem, *[vmem] * 5], [block, *halves], cost=apply_cost
        )(kept, vector, *summed(mine, theirs), left_env, right_env)

    incoming, edge, second_vector, turned = call(
        unpack,
        [smem, smem, vmem, vmem, vmem],
        [shape(terms, states, states), shape(states, states), block, shape(states, states)],
        (),
    )(kept, mpo_gain, left_env, package, psi_two)

    first_rows, site, mine, theirs = call(
        second_start,
        [smem, *[vmem] * 7],
        [rows, shape(states, states), *halves],
        cost=apply_cost,
    )(kept, vector, *summed(mine, theirs), turned, edge, incoming, right_env)
    vector = second_vector
    for _ in range(ITERS - 1):
        vector, mine, theirs = call(
            second_step, [smem, *[vmem] * 7], [block, *halves], cost=apply_cost
        )(kept, vector, *summed(mine, theirs), site, edge, incoming, right_env)
    (second_rows,) = call(second_end, [smem, *[vmem] * 3], [rows])(
        kept, vector, *summed(mine, theirs)
    )
    return first_rows, second_rows


def solution(mesh):
    placed = (
        P("seg", "sec", None, None),
        P("seg", "sec", None, None),
        P("seg", None, None),
        P("seg", None, None),
        P("seg", None, None),
        P("seg", "sec"),
        P("seg", None),
    )
    return jax.shard_map(
        on_device,
        mesh=mesh,
        in_specs=placed,
        out_specs=(P("seg", "sec", None), P("seg", "sec", None)),
        check_vma=False,
    )
```

```python
import functools

import jax
import jax.numpy as jnp
from jax import lax
from jax.experimental import pallas as pl
from jax.experimental.pallas import tpu as pltpu
from jax.sharding import PartitionSpec as P

ITERS = 3
EPSILON = 1e-06
DESCENT = 0.3
CHUNK = 5
MIB = 1024 * 1024

F32 = jnp.float32
BF16 = jnp.bfloat16


def dot(a, b, dims=((1,), (0,))):
    return lax.dot_general(a, b, (dims, ((), ())), preferred_element_type=F32)


def live_rows(shape, live):
    return lax.broadcasted_iota(jnp.int32, shape, 0) < live


def begun(start, live):
    states = start.shape[-1]
    block = start[...].reshape(states, states).astype(F32)
    block = jnp.where(live_rows(block.shape, live), block, 0.0)
    return block * (states / jnp.sqrt(jnp.sum(block * block) + EPSILON))


def joined(mine, other, live):
    low = lax.rem(lax.axis_index("sec"), 2) == 0
    own, far = mine[...].astype(F32), other[...].astype(F32)
    product = jnp.concatenate([jnp.where(low, own, far), jnp.where(low, far, own)], axis=0)
    return jnp.where(live_rows(product.shape, live), product, 0.0)


def coefficients(current, product):
    states = current.shape[0]
    xx, xy = jnp.sum(current * current), jnp.sum(current * product)
    yy = jnp.sum(product * product)
    energy = xy / xx
    norm = xx + DESCENT * DESCENT * jnp.maximum(yy - energy * xy, 0.0)
    scale = states / jnp.sqrt(norm + EPSILON)
    return scale * (1.0 + DESCENT * energy), -DESCENT * scale


def stepped(vector, mine, other, live):
    current, product = vector[...], joined(mine, other, live)
    a, b = coefficients(current, product)
    return a * current + b * product


def own_rows(block, rows):
    share = rows.shape[1]
    rows[0] = block[pl.ds(pl.multiple_of(lax.axis_index("sec") * share, share), share), :]


def contract(vector, left, right, acc):
    states = vector.shape[0]
    terms = left.shape[0]
    chunk = CHUNK if terms % CHUNK == 0 else 1
    for first in range(0, terms, chunk):
        inner = dot(left[first : first + chunk].reshape(chunk * states, states), vector)
        total = None
        for n in range(chunk):
            part = dot(inner[n * states : (n + 1) * states].astype(BF16), right[first + n])
            total = part if total is None else total + part
        if first == 0:
            acc[...] = total
        else:
            acc[...] += total


def hand_out(acc, mine, theirs):
    half = mine.shape[0]
    core = lax.rem(lax.axis_index("sec"), 2)
    mine[...] = acc[pl.ds(pl.multiple_of(core * half, half), half), :].astype(BF16)
    theirs[...] = acc[pl.ds(pl.multiple_of((1 - core) * half, half), half), :].astype(BF16)


def first_start(kept, start, left, right, vector, mine, theirs, applied, acc):
    states = start.shape[2]
    block = jnp.where(live_rows((states, states), kept[0, 0]), start[0].astype(F32), 0.0)
    scale = states / jnp.sqrt(jnp.sum(block * block) + EPSILON)
    vector[...] = block * scale
    contract(block.astype(BF16), left.at[0], right.at[0], acc)
    applied[...] = acc[...] * scale
    hand_out(applied, mine, theirs)


def first_step(
    kept, vector, applied, summed, other, left, right, after, mine, theirs, applied_after, acc
):
    current, product = vector[...], joined(summed, other, kept[0, 0])
    a, b = coefficients(current, product)
    contract(product.astype(BF16), left.at[0], right.at[0], acc)
    after[...] = a * current + b * product
    applied_after[...] = a * applied[...] + b * acc[...]
    hand_out(applied_after, mine, theirs)


def place(shape):
    return lax.broadcasted_iota(jnp.int32, shape, 0), lax.broadcasted_iota(jnp.int32, shape, 1)


def pack(gain, left, edge, ready, package):
    terms, states = left.shape[1], left.shape[2]
    row, column = place((states, states))
    pairs = terms // 2

    def scaled(n):
        return left[0, n].astype(F32) * gain[0, n]

    for n in range(pairs):
        second = scaled(2 * n + 1)
        slab = jnp.where(row >= column, scaled(2 * n), second)
        package[n * states : (n + 1) * states] = slab.astype(BF16)
        diagonal = jnp.sum(jnp.where(row == column, second, 0.0), axis=0, keepdims=True)
        base = (pairs + terms % 2 + 1) * states + 16 * n
        package[base : base + 16] = jnp.broadcast_to(diagonal, (16, states)).astype(BF16)
    if terms % 2:
        package[pairs * states : (pairs + 1) * states] = scaled(terms - 1).astype(BF16)
    last = pairs + terms % 2
    package[last * states : (last + 1) * states] = edge[0]


def unpack(kept, gain, left, package, start, incoming, site, vector, turned):
    terms, states = left.shape[1], left.shape[2]
    row, column = place((states, states))
    pairs = terms // 2
    at_start = lax.axis_index("seg") == 0

    @pl.when(at_start)
    def _():
        for n in range(terms):
            incoming[n] = (left[0, n].astype(F32) * gain[0, n]).astype(BF16)
        site[...] = jnp.where(row == column, 1.0, 0.0).astype(BF16)

    @pl.when(jnp.logical_not(at_start))
    def _():
        for n in range(pairs):
            slab = package[n * states : (n + 1) * states].astype(F32)
            mirrored = slab.T
            base = (pairs + terms % 2 + 1) * states + 16 * n
            diagonal = package[base : base + 16].astype(F32)[0:1]
            one = jnp.where(row >= column, slab, mirrored)
            two = jnp.where(row < column, slab, jnp.where(row == column, diagonal, mirrored))
            incoming[2 * n] = (one * gain[0, 2 * n]).astype(BF16)
            incoming[2 * n + 1] = (two * gain[0, 2 * n + 1]).astype(BF16)
        if terms % 2:
            slab = package[pairs * states : (pairs + 1) * states].astype(F32)
            incoming[terms - 1] = (slab * gain[0, terms - 1]).astype(BF16)
        last = pairs + terms % 2
        site[...] = package[last * states : (last + 1) * states]

    current = begun(start, kept[0, 1])
    vector[...] = current
    turned[...] = dot(site[...], current.astype(BF16)).astype(BF16)


def second_apply(inner, edge, site, incoming, right, acc):
    contract(inner, incoming, right.at[0], acc)
    outer = dot(acc[...].astype(BF16), site, ((1,), (1,))).astype(BF16)
    return dot(edge[...], outer, ((0,), (0,)))


def second_start(
    kept, vector, summed, other, turned, edge, incoming, right, rows, site, mine, theirs, applied, acc
):
    states = vector.shape[1]
    acc[...] = stepped(vector, summed, other, kept[0, 0])
    own_rows(acc, rows)
    site_left = (acc[...] * states**-0.5).astype(BF16)
    site[...] = site_left
    inner = dot(turned[...], site_left).astype(BF16)
    applied[...] = second_apply(inner, edge, site_left, incoming, right, acc)
    hand_out(applied, mine, theirs)


def second_step(
    kept, vector, applied, summed, other, site, edge, incoming, right,
    after, mine, theirs, applied_after, acc,
):
    current, product = vector[...], joined(summed, other, kept[0, 1])
    a, b = coefficients(current, product)
    inner = dot(product.astype(BF16), site[...]).astype(BF16)
    inner = dot(edge[...], inner).astype(BF16)
    found = second_apply(inner, edge, site[...], incoming, right, acc)
    after[...] = a * current + b * product
    applied_after[...] = a * applied[...] + b * found
    hand_out(applied_after, mine, theirs)


def second_end(kept, vector, summed, other, rows, acc):
    acc[...] = stepped(vector, summed, other, kept[0, 1])
    own_rows(acc, rows)


def add(count, *refs):
    total = refs[0][...].astype(F32)
    for ref in refs[1:count]:
        total = total + ref[...].astype(F32)
    refs[-1][...] = total.astype(BF16)


def on_device(left_env, right_env, edge_site, psi_one, psi_two, mpo_gain, kept):
    terms, states = left_env.shape[1], left_env.shape[2]
    sections, segments = lax.axis_size("sec"), lax.axis_size("seg")
    share, half = states // sections, states // 2

    smem = pl.BlockSpec(memory_space=pltpu.SMEM)
    vmem = pl.BlockSpec(memory_space=pltpu.VMEM)

    def shape(*dims, dtype=BF16):
        return jax.ShapeDtypeStruct(dims, dtype)

    block = shape(states, states, dtype=F32)
    halves = [shape(half, states)] * 2
    rows = shape(1, share, states, dtype=F32)
    acc = pltpu.VMEM((states, states), F32)
    apply_cost = pl.CostEstimate(
        flops=4 * terms * states**3, bytes_accessed=4 * terms * states**2, transcendentals=0
    )

    def call(kernel, ins, outs, scratch=(acc,), limit=12 * MIB, cost=None, name=None):
        return pl.pallas_call(
            kernel,
            in_specs=ins,
            out_specs=[vmem] * len(outs),
            out_shape=outs,
            scratch_shapes=list(scratch),
            compiler_params=pltpu.CompilerParams(vmem_limit_bytes=limit),
            cost_estimate=cost,
            name=name or kernel.__name__,
        )

    def step_call(kernel, count, step):
        outs, scratch = [block, *halves], [acc]
        if step < ITERS - 2:
            outs.append(block)
        else:
            scratch.insert(0, acc)
        return call(kernel, [smem, *[vmem] * count], outs, scratch, cost=apply_cost)

    def moved(value, target):
        return lax.ppermute(value, "sec", [(n, target(n) % sections) for n in range(sections)])

    def added(*values, after=()):
        kernel = functools.partial(add, len(values))
        specs = [vmem] * (len(values) + len(after))
        return call(kernel, specs, halves[:1], (), 2 * MIB, name="add")(*values, *after)[0]

    def between(chip):
        count = sections // 2
        return lambda n: 2 * (chip(n // 2, 1 if n // 2 % 2 else -1) % count) + n % 2

    near = [between(lambda z, up, far=far: z + up * far) for far in (2, 1, 3)]

    def summed(mine, theirs, after=(), beside=None):
        total = added(mine, moved(theirs, lambda n: n ^ 1))
        if beside is not None:
            beside(total)
        total = added(total, moved(total, lambda n: n ^ 2))
        parts = [moved(total, target) for target in near]
        total = added(total, *parts, after=after)
        return total, moved(total, lambda n: n ^ 1)

    blocks = shape(terms, states, states)
    left, right = left_env, right_env
    vector, mine, theirs, *applied = call(
        first_start, [smem, *[vmem] * 3], [block, *halves, block], cost=apply_cost
    )(kept, psi_one, left, right)

    slabs = terms // 2 + terms % 2 + 1
    sent = []

    def hand_over(ready):
        (package,) = call(
            pack,
            [smem, vmem, vmem, vmem],
            [shape(slabs * states + 16 * (terms // 2), states)],
            (),
        )(mpo_gain, left, edge_site, ready)
        sent.append(lax.ppermute(package, "seg", [(n, n + 1) for n in range(segments - 1)]))

    for step in range(ITERS - 1):
        total = summed(mine, theirs, beside=None if step else hand_over)
        vector, mine, theirs, *applied = step_call(first_step, 6, step)(
            kept, vector, *applied, *total, left, right
        )

    incoming, edge, second_vector, turned = call(
        unpack,
        [smem, smem, vmem, vmem, vmem],
        [blocks, shape(states, states), block, shape(states, states)],
        (),
    )(kept, mpo_gain, left, sent[0], psi_two)

    first_rows, site, mine, theirs, *applied = call(
        second_start,
        [smem, *[vmem] * 7],
        [rows, shape(states, states), *halves, block],
        cost=apply_cost,
    )(kept, vector, *summed(mine, theirs, (turned,)), turned, edge, incoming, right)
    vector = second_vector
    for step in range(ITERS - 1):
        total = summed(mine, theirs)
        vector, mine, theirs, *applied = step_call(second_step, 8, step)(
            kept, vector, *applied, *total, site, edge, incoming, right
        )
    (second_rows,) = call(second_end, [smem, *[vmem] * 3], [rows])(
        kept, vector, *summed(mine, theirs)
    )
    return first_rows, second_rows


def solution(mesh):
    placed = (
        P("seg", "sec", None, None),
        P("seg", "sec", None, None),
        P("seg", None, None),
        P("seg", None, None),
        P("seg", None, None),
        P("seg", "sec"),
        P("seg", None),
    )
    return jax.shard_map(
        on_device,
        mesh=mesh,
        in_specs=placed,
        out_specs=(P("seg", "sec", None), P("seg", "sec", None)),
        check_vma=False,
    )
```

```python
import functools

import jax
import jax.numpy as jnp
from jax import lax
from jax.experimental import pallas as pl
from jax.experimental.pallas import tpu as pltpu
from jax.sharding import PartitionSpec as P

ITERS = 3
EPSILON = 1e-06
DESCENT = 0.3
CHUNK = 5
MIB = 1024 * 1024
GATHERED = True

F32 = jnp.float32
BF16 = jnp.bfloat16


def dot(a, b, dims=((1,), (0,))):
    return lax.dot_general(a, b, (dims, ((), ())), preferred_element_type=F32)


def live_rows(shape, live):
    return lax.broadcasted_iota(jnp.int32, shape, 0) < live


def begun(start, live):
    states = start.shape[-1]
    block = start[...].reshape(states, states).astype(F32)
    block = jnp.where(live_rows(block.shape, live), block, 0.0)
    return block * (states / jnp.sqrt(jnp.sum(block * block) + EPSILON))


def joined(summed, live):
    if len(summed) == 1:
        states = summed[0].shape[2]
        product = summed[0][...].reshape(states, states).astype(F32)
    else:
        low = lax.rem(lax.axis_index("sec"), 2) == 0
        own, far = summed[0][...].astype(F32), summed[1][...].astype(F32)
        product = jnp.concatenate([jnp.where(low, own, far), jnp.where(low, far, own)], axis=0)
    return jnp.where(live_rows(product.shape, live), product, 0.0)


def coefficients(current, product):
    states = current.shape[0]
    xx, xy = jnp.sum(current * current), jnp.sum(current * product)
    yy = jnp.sum(product * product)
    energy = xy / xx
    norm = xx + DESCENT * DESCENT * jnp.maximum(yy - energy * xy, 0.0)
    scale = states / jnp.sqrt(norm + EPSILON)
    return scale * (1.0 + DESCENT * energy), -DESCENT * scale


def stepped(vector, summed, live):
    current, product = vector[...], joined(summed, live)
    a, b = coefficients(current, product)
    return a * current + b * product


def own_rows(block, rows):
    share = rows.shape[1]
    rows[0] = block[pl.ds(pl.multiple_of(lax.axis_index("sec") * share, share), share), :]


def contract(vector, left, right, acc):
    states = vector.shape[0]
    terms = left.shape[0]
    chunk = CHUNK if terms % CHUNK == 0 else 1
    for first in range(0, terms, chunk):
        inner = dot(left[first : first + chunk].reshape(chunk * states, states), vector)
        total = None
        for n in range(chunk):
            part = dot(inner[n * states : (n + 1) * states].astype(BF16), right[first + n])
            total = part if total is None else total + part
        if first == 0:
            acc[...] = total
        else:
            acc[...] += total


def hand_out(acc, mine, theirs):
    half = mine.shape[0]
    core = lax.rem(lax.axis_index("sec"), 2)
    mine[...] = acc[pl.ds(pl.multiple_of(core * half, half), half), :].astype(BF16)
    theirs[...] = acc[pl.ds(pl.multiple_of((1 - core) * half, half), half), :].astype(BF16)


def first_start(kept, start, left, right, vector, mine, theirs, applied, acc):
    states = start.shape[2]
    block = jnp.where(live_rows((states, states), kept[0, 0]), start[0].astype(F32), 0.0)
    scale = states / jnp.sqrt(jnp.sum(block * block) + EPSILON)
    vector[...] = block * scale
    contract(block.astype(BF16), left.at[0], right.at[0], acc)
    applied[...] = acc[...] * scale
    hand_out(applied, mine, theirs)


def first_step(
    kept, vector, applied, summed, left, right, after, mine, theirs, applied_after, acc
):
    current, product = vector[...], joined(summed, kept[0, 0])
    a, b = coefficients(current, product)
    contract(product.astype(BF16), left.at[0], right.at[0], acc)
    after[...] = a * current + b * product
    applied_after[...] = a * applied[...] + b * acc[...]
    hand_out(applied_after, mine, theirs)


def place(shape):
    return lax.broadcasted_iota(jnp.int32, shape, 0), lax.broadcasted_iota(jnp.int32, shape, 1)


def pack(gain, left, edge, ready, package):
    terms, states = left.shape[1], left.shape[2]
    row, column = place((states, states))
    pairs = terms // 2

    def scaled(n):
        return left[0, n].astype(F32) * gain[0, n]

    for n in range(pairs):
        second = scaled(2 * n + 1)
        slab = jnp.where(row >= column, scaled(2 * n), second)
        package[n * states : (n + 1) * states] = slab.astype(BF16)
        diagonal = jnp.sum(jnp.where(row == column, second, 0.0), axis=0, keepdims=True)
        base = (pairs + terms % 2 + 1) * states + 16 * n
        package[base : base + 16] = jnp.broadcast_to(diagonal, (16, states)).astype(BF16)
    if terms % 2:
        package[pairs * states : (pairs + 1) * states] = scaled(terms - 1).astype(BF16)
    last = pairs + terms % 2
    package[last * states : (last + 1) * states] = edge[0]


def unpack(kept, gain, left, package, start, incoming, site, vector, turned):
    terms, states = left.shape[1], left.shape[2]
    row, column = place((states, states))
    pairs = terms // 2
    at_start = lax.axis_index("seg") == 0

    @pl.when(at_start)
    def _():
        for n in range(terms):
            incoming[n] = (left[0, n].astype(F32) * gain[0, n]).astype(BF16)
        site[...] = jnp.where(row == column, 1.0, 0.0).astype(BF16)

    @pl.when(jnp.logical_not(at_start))
    def _():
        for n in range(pairs):
            slab = package[n * states : (n + 1) * states].astype(F32)
            mirrored = slab.T
            base = (pairs + terms % 2 + 1) * states + 16 * n
            diagonal = package[base : base + 16].astype(F32)[0:1]
            one = jnp.where(row >= column, slab, mirrored)
            two = jnp.where(row < column, slab, jnp.where(row == column, diagonal, mirrored))
            incoming[2 * n] = (one * gain[0, 2 * n]).astype(BF16)
            incoming[2 * n + 1] = (two * gain[0, 2 * n + 1]).astype(BF16)
        if terms % 2:
            slab = package[pairs * states : (pairs + 1) * states].astype(F32)
            incoming[terms - 1] = (slab * gain[0, terms - 1]).astype(BF16)
        last = pairs + terms % 2
        site[...] = package[last * states : (last + 1) * states]

    current = begun(start, kept[0, 1])
    vector[...] = current
    turned[...] = dot(site[...], current.astype(BF16)).astype(BF16)


def second_apply(inner, edge, site, incoming, right, acc):
    contract(inner, incoming, right.at[0], acc)
    outer = dot(acc[...].astype(BF16), site, ((1,), (1,))).astype(BF16)
    return dot(edge[...], outer, ((0,), (0,)))


def second_start(
    kept, vector, summed, turned, edge, incoming, right, rows, site, mine, theirs, applied, acc
):
    states = vector.shape[1]
    acc[...] = stepped(vector, summed, kept[0, 0])
    own_rows(acc, rows)
    site_left = (acc[...] * states**-0.5).astype(BF16)
    site[...] = site_left
    inner = dot(turned[...], site_left).astype(BF16)
    applied[...] = second_apply(inner, edge, site_left, incoming, right, acc)
    hand_out(applied, mine, theirs)


def second_step(
    kept, vector, applied, summed, site, edge, incoming, right,
    after, mine, theirs, applied_after, acc,
):
    current, product = vector[...], joined(summed, kept[0, 1])
    a, b = coefficients(current, product)
    inner = dot(product.astype(BF16), site[...]).astype(BF16)
    inner = dot(edge[...], inner).astype(BF16)
    found = second_apply(inner, edge, site[...], incoming, right, acc)
    after[...] = a * current + b * product
    applied_after[...] = a * applied[...] + b * found
    hand_out(applied_after, mine, theirs)


def second_end(kept, vector, summed, rows, acc):
    acc[...] = stepped(vector, summed, kept[0, 1])
    own_rows(acc, rows)


def add(count, *refs):
    total = refs[0][...].astype(F32)
    for ref in refs[1:count]:
        total = total + ref[...].astype(F32)
    refs[-1][...] = total.astype(BF16)


def on_device(left_env, right_env, edge_site, psi_one, psi_two, mpo_gain, kept):
    terms, states = left_env.shape[1], left_env.shape[2]
    sections, segments = lax.axis_size("sec"), lax.axis_size("seg")
    share, half = states // sections, states // 2

    smem = pl.BlockSpec(memory_space=pltpu.SMEM)
    vmem = pl.BlockSpec(memory_space=pltpu.VMEM)

    def shape(*dims, dtype=BF16):
        return jax.ShapeDtypeStruct(dims, dtype)

    block = shape(states, states, dtype=F32)
    halves = [shape(half, states)] * 2
    rows = shape(1, share, states, dtype=F32)
    acc = pltpu.VMEM((states, states), F32)
    apply_cost = pl.CostEstimate(
        flops=4 * terms * states**3, bytes_accessed=4 * terms * states**2, transcendentals=0
    )

    def call(kernel, ins, outs, scratch=(acc,), limit=12 * MIB, cost=None, name=None):
        return pl.pallas_call(
            kernel,
            in_specs=ins,
            out_specs=[vmem] * len(outs),
            out_shape=outs,
            scratch_shapes=list(scratch),
            compiler_params=pltpu.CompilerParams(vmem_limit_bytes=limit),
            cost_estimate=cost,
            name=name or kernel.__name__,
        )

    def step_call(kernel, before, total, after, step):
        outs, scratch = [block, *halves], [acc]
        if step < ITERS - 2:
            outs.append(block)
        else:
            scratch.insert(0, acc)
        specs = [smem, *[vmem] * len(before), tuple(vmem for _ in total), *[vmem] * len(after)]
        return call(kernel, specs, outs, scratch, cost=apply_cost)(kept, *before, total, *after)

    def moved(value, target):
        return lax.ppermute(value, "sec", [(n, target(n) % sections) for n in range(sections)])

    def added(*values, after=()):
        kernel = functools.partial(add, len(values))
        specs = [vmem] * (len(values) + len(after))
        return call(kernel, specs, halves[:1], (), 2 * MIB, name="add")(*values, *after)[0]

    def between(chip):
        count = sections // 2
        return lambda n: 2 * (chip(n // 2, 1 if n // 2 % 2 else -1) % count) + n % 2

    cores = [[n, n + 1] for n in range(0, sections, 2)]
    near = [between(lambda z, up, far=far: z + up * far) for far in (2, 1, 3)]

    def summed(mine, theirs, after=(), beside=None, gathered=GATHERED):
        total = added(mine, moved(theirs, lambda n: n ^ 1))
        if beside is not None:
            beside(total)
        total = added(total, moved(total, lambda n: n ^ 2))
        parts = [moved(total, target) for target in near]
        total = added(total, *parts, after=after)
        if gathered:
            return (lax.all_gather(total, "sec", axis=0, axis_index_groups=cores),)
        return total, moved(total, lambda n: n ^ 1)

    blocks = shape(terms, states, states)
    left, right = left_env, right_env
    vector, mine, theirs, *applied = call(
        first_start, [smem, *[vmem] * 3], [block, *halves, block], cost=apply_cost
    )(kept, psi_one, left, right)

    slabs = terms // 2 + terms % 2 + 1
    sent = []

    def hand_over(ready):
        (package,) = call(
            pack,
            [smem, vmem, vmem, vmem],
            [shape(slabs * states + 16 * (terms // 2), states)],
            (),
        )(mpo_gain, left, edge_site, ready)
        sent.append(lax.ppermute(package, "seg", [(n, n + 1) for n in range(segments - 1)]))

    for step in range(ITERS - 1):
        total = summed(mine, theirs, beside=None if step else hand_over)
        vector, mine, theirs, *applied = step_call(
            first_step, (vector, *applied), total, (left, right), step
        )

    incoming, edge, second_vector, turned = call(
        unpack,
        [smem, smem, vmem, vmem, vmem],
        [blocks, shape(states, states), block, shape(states, states)],
        (),
    )(kept, mpo_gain, left, sent[0], psi_two)

    total = summed(mine, theirs, (turned,))
    first_rows, site, mine, theirs, *applied = call(
        second_start,
        [smem, vmem, tuple(vmem for _ in total), *[vmem] * 4],
        [rows, shape(states, states), *halves, block],
        cost=apply_cost,
    )(kept, vector, total, turned, edge, incoming, right)
    vector = second_vector
    for step in range(ITERS - 1):
        total = summed(mine, theirs)
        vector, mine, theirs, *applied = step_call(
            second_step, (vector, *applied), total, (site, edge, incoming, right), step
        )
    total = summed(mine, theirs, gathered=True)
    (second_rows,) = call(second_end, [smem, vmem, tuple(vmem for _ in total)], [rows])(
        kept, vector, total
    )
    return first_rows, second_rows


def solution(mesh):
    placed = (
        P("seg", "sec", None, None),
        P("seg", "sec", None, None),
        P("seg", None, None),
        P("seg", None, None),
        P("seg", None, None),
        P("seg", "sec"),
        P("seg", None),
    )
    return jax.shard_map(
        on_device,
        mesh=mesh,
        in_specs=placed,
        out_specs=(P("seg", "sec", None), P("seg", "sec", None)),
        check_vma=False,
    )
```

```python
import functools

import jax
import jax.numpy as jnp
from jax import lax
from jax.experimental import pallas as pl
from jax.experimental.pallas import tpu as pltpu
from jax.sharding import PartitionSpec as P

ITERS = 3
EPSILON = 1e-06
DESCENT = 0.3
CHUNK = 5
MIB = 1024 * 1024
GATHERED = True

F32 = jnp.float32
BF16 = jnp.bfloat16


def dot(a, b, dims=((1,), (0,))):
    return lax.dot_general(a, b, (dims, ((), ())), preferred_element_type=F32)


def live_rows(shape, live):
    return lax.broadcasted_iota(jnp.int32, shape, 0) < live


def begun(start, live):
    states = start.shape[-1]
    block = start[...].reshape(states, states).astype(F32)
    block = jnp.where(live_rows(block.shape, live), block, 0.0)
    return block * (states / jnp.sqrt(jnp.sum(block * block) + EPSILON))


def joined(summed, live):
    if len(summed) == 1:
        states = summed[0].shape[2]
        product = summed[0][...].reshape(states, states).astype(F32)
    else:
        low = lax.rem(lax.axis_index("sec"), 2) == 0
        own, far = summed[0][...].astype(F32), summed[1][...].astype(F32)
        product = jnp.concatenate([jnp.where(low, own, far), jnp.where(low, far, own)], axis=0)
    return jnp.where(live_rows(product.shape, live), product, 0.0)


def coefficients(current, product):
    states = current.shape[0]
    xx, xy = jnp.sum(current * current), jnp.sum(current * product)
    yy = jnp.sum(product * product)
    energy = xy / xx
    norm = xx + DESCENT * DESCENT * jnp.maximum(yy - energy * xy, 0.0)
    scale = states / jnp.sqrt(norm + EPSILON)
    return scale * (1.0 + DESCENT * energy), -DESCENT * scale


def stepped(vector, summed, live):
    current, product = vector[...], joined(summed, live)
    a, b = coefficients(current, product)
    return a * current + b * product


def own_rows(block, rows):
    share = rows.shape[1]
    rows[0] = block[pl.ds(pl.multiple_of(lax.axis_index("sec") * share, share), share), :]


def contract(vector, left, right, acc):
    states = vector.shape[0]
    terms = left.shape[0]
    chunk = CHUNK if terms % CHUNK == 0 else 1
    for first in range(0, terms, chunk):
        inner = dot(left[first : first + chunk].reshape(chunk * states, states), vector)
        total = None
        for n in range(chunk):
            part = dot(inner[n * states : (n + 1) * states].astype(BF16), right[first + n])
            total = part if total is None else total + part
        if first == 0:
            acc[...] = total
        else:
            acc[...] += total


def hand_out(acc, mine, theirs):
    half = mine.shape[0]
    core = lax.rem(lax.axis_index("sec"), 2)
    mine[...] = acc[pl.ds(pl.multiple_of(core * half, half), half), :].astype(BF16)
    theirs[...] = acc[pl.ds(pl.multiple_of((1 - core) * half, half), half), :].astype(BF16)


def first_start(kept, start, left, right, vector, mine, theirs, applied, acc):
    states = start.shape[2]
    block = jnp.where(live_rows((states, states), kept[0, 0]), start[0].astype(F32), 0.0)
    scale = states / jnp.sqrt(jnp.sum(block * block) + EPSILON)
    vector[...] = block * scale
    contract(block.astype(BF16), left.at[0], right.at[0], acc)
    applied[...] = acc[...] * scale
    hand_out(applied, mine, theirs)


def first_step(
    kept, vector, applied, summed, left, right, after, mine, theirs, applied_after, acc
):
    current, product = vector[...], joined(summed, kept[0, 0])
    a, b = coefficients(current, product)
    contract(product.astype(BF16), left.at[0], right.at[0], acc)
    after[...] = a * current + b * product
    applied_after[...] = a * applied[...] + b * acc[...]
    hand_out(applied_after, mine, theirs)


def place(shape):
    return lax.broadcasted_iota(jnp.int32, shape, 0), lax.broadcasted_iota(jnp.int32, shape, 1)


def pack(gain, left, edge, package):
    terms, states = left.shape[1], left.shape[2]
    row, column = place((states, states))
    pairs = terms // 2

    def scaled(n):
        return left[0, n].astype(F32) * gain[0, n]

    for n in range(pairs):
        second = scaled(2 * n + 1)
        slab = jnp.where(row >= column, scaled(2 * n), second)
        package[n * states : (n + 1) * states] = slab.astype(BF16)
        diagonal = jnp.sum(jnp.where(row == column, second, 0.0), axis=0, keepdims=True)
        base = (pairs + terms % 2 + 1) * states + 16 * n
        package[base : base + 16] = jnp.broadcast_to(diagonal, (16, states)).astype(BF16)
    if terms % 2:
        package[pairs * states : (pairs + 1) * states] = scaled(terms - 1).astype(BF16)
    last = pairs + terms % 2
    package[last * states : (last + 1) * states] = edge[0]


def unpack(kept, gain, left, package, start, incoming, site, vector, turned):
    terms, states = left.shape[1], left.shape[2]
    row, column = place((states, states))
    pairs = terms // 2
    at_start = lax.axis_index("seg") == 0

    @pl.when(at_start)
    def _():
        for n in range(terms):
            incoming[n] = (left[0, n].astype(F32) * gain[0, n]).astype(BF16)
        site[...] = jnp.where(row == column, 1.0, 0.0).astype(BF16)

    @pl.when(jnp.logical_not(at_start))
    def _():
        for n in range(pairs):
            slab = package[n * states : (n + 1) * states].astype(F32)
            mirrored = slab.T
            base = (pairs + terms % 2 + 1) * states + 16 * n
            diagonal = package[base : base + 16].astype(F32)[0:1]
            one = jnp.where(row >= column, slab, mirrored)
            two = jnp.where(row < column, slab, jnp.where(row == column, diagonal, mirrored))
            incoming[2 * n] = (one * gain[0, 2 * n]).astype(BF16)
            incoming[2 * n + 1] = (two * gain[0, 2 * n + 1]).astype(BF16)
        if terms % 2:
            slab = package[pairs * states : (pairs + 1) * states].astype(F32)
            incoming[terms - 1] = (slab * gain[0, terms - 1]).astype(BF16)
        last = pairs + terms % 2
        site[...] = package[last * states : (last + 1) * states]

    current = begun(start, kept[0, 1])
    vector[...] = current
    turned[...] = dot(site[...], current.astype(BF16)).astype(BF16)


def second_apply(inner, edge, site, incoming, right, acc):
    contract(inner, incoming, right.at[0], acc)
    outer = dot(acc[...].astype(BF16), site, ((1,), (1,))).astype(BF16)
    return dot(edge[...], outer, ((0,), (0,)))


def second_start(
    kept, vector, summed, turned, edge, incoming, right, rows, site, mine, theirs, applied, acc
):
    states = vector.shape[1]
    acc[...] = stepped(vector, summed, kept[0, 0])
    own_rows(acc, rows)
    site_left = (acc[...] * states**-0.5).astype(BF16)
    site[...] = site_left
    inner = dot(turned[...], site_left).astype(BF16)
    applied[...] = second_apply(inner, edge, site_left, incoming, right, acc)
    hand_out(applied, mine, theirs)


def second_step(
    kept, vector, applied, summed, site, edge, incoming, right,
    after, mine, theirs, applied_after, acc,
):
    current, product = vector[...], joined(summed, kept[0, 1])
    a, b = coefficients(current, product)
    inner = dot(product.astype(BF16), site[...]).astype(BF16)
    inner = dot(edge[...], inner).astype(BF16)
    found = second_apply(inner, edge, site[...], incoming, right, acc)
    after[...] = a * current + b * product
    applied_after[...] = a * applied[...] + b * found
    hand_out(applied_after, mine, theirs)


def second_end(kept, vector, summed, rows):
    live, share, half = kept[0, 1], rows.shape[1], summed[0].shape[1]
    a, b = coefficients(vector[...], joined(summed, live))
    start = lax.axis_index("sec") * share
    part = pl.ds(pl.multiple_of(lax.rem(start, half), share), share)
    product = summed[0][lax.div(start, half), part, :].astype(F32)
    product = jnp.where(live_rows(product.shape, live - start), product, 0.0)
    rows[0] = a * vector[pl.ds(pl.multiple_of(start, share), share), :] + b * product


def add(count, *refs):
    total = refs[0][...].astype(F32)
    for ref in refs[1:count]:
        total = total + ref[...].astype(F32)
    refs[-1][...] = total.astype(BF16)


def on_device(left_env, right_env, edge_site, psi_one, psi_two, mpo_gain, kept):
    terms, states = left_env.shape[1], left_env.shape[2]
    sections, segments = lax.axis_size("sec"), lax.axis_size("seg")
    share, half = states // sections, states // 2

    smem = pl.BlockSpec(memory_space=pltpu.SMEM)
    vmem = pl.BlockSpec(memory_space=pltpu.VMEM)

    def shape(*dims, dtype=BF16):
        return jax.ShapeDtypeStruct(dims, dtype)

    block = shape(states, states, dtype=F32)
    halves = [shape(half, states)] * 2
    rows = shape(1, share, states, dtype=F32)
    acc = pltpu.VMEM((states, states), F32)
    apply_cost = pl.CostEstimate(
        flops=4 * terms * states**3, bytes_accessed=4 * terms * states**2, transcendentals=0
    )

    def call(kernel, ins, outs, scratch=(acc,), limit=12 * MIB, cost=None, name=None):
        return pl.pallas_call(
            kernel,
            in_specs=ins,
            out_specs=[vmem] * len(outs),
            out_shape=outs,
            scratch_shapes=list(scratch),
            compiler_params=pltpu.CompilerParams(vmem_limit_bytes=limit),
            cost_estimate=cost,
            name=name or kernel.__name__,
        )

    def step_call(kernel, before, total, after, step):
        outs, scratch = [block, *halves], [acc]
        if step < ITERS - 2:
            outs.append(block)
        else:
            scratch.insert(0, acc)
        specs = [smem, *[vmem] * len(before), tuple(vmem for _ in total), *[vmem] * len(after)]
        return call(kernel, specs, outs, scratch, cost=apply_cost)(kept, *before, total, *after)

    def moved(value, target):
        return lax.ppermute(value, "sec", [(n, target(n) % sections) for n in range(sections)])

    def added(*values, after=()):
        kernel = functools.partial(add, len(values))
        specs = [vmem] * (len(values) + len(after))
        return call(kernel, specs, halves[:1], (), 2 * MIB, name="add")(*values, *after)[0]

    def between(chip):
        count = sections // 2
        return lambda n: 2 * (chip(n // 2, 1 if n // 2 % 2 else -1) % count) + n % 2

    cores = [[n, n + 1] for n in range(0, sections, 2)]
    near = [between(lambda z, up, far=far: z + up * far) for far in (2, 1, 3)]

    def summed(mine, theirs, after=(), gathered=GATHERED):
        total = added(mine, moved(theirs, lambda n: n ^ 1))
        total = added(total, moved(total, lambda n: n ^ 2))
        parts = [moved(total, target) for target in near]
        total = added(total, *parts, after=after)
        if gathered:
            return (lax.all_gather(total, "sec", axis=0, axis_index_groups=cores),)
        return total, moved(total, lambda n: n ^ 1)

    blocks = shape(terms, states, states)
    left, right = left_env, right_env
    slabs = terms // 2 + terms % 2 + 1
    (package,) = call(
        pack,
        [smem, vmem, vmem],
        [shape(slabs * states + 16 * (terms // 2), states)],
        (),
        cost=pl.CostEstimate(
            flops=60 * terms * states**3, bytes_accessed=4 * terms * states**2, transcendentals=0
        ),
    )(mpo_gain, left_env, edge_site)
    package = lax.ppermute(package, "seg", [(n, n + 1) for n in range(segments - 1)])

    vector, mine, theirs, *applied = call(
        first_start, [smem, *[vmem] * 3], [block, *halves, block], cost=apply_cost
    )(kept, psi_one, left, right)

    for step in range(ITERS - 1):
        total = summed(mine, theirs)
        vector, mine, theirs, *applied = step_call(
            first_step, (vector, *applied), total, (left, right), step
        )

    incoming, edge, second_vector, turned = call(
        unpack,
        [smem, smem, vmem, vmem, vmem],
        [blocks, shape(states, states), block, shape(states, states)],
        (),
    )(kept, mpo_gain, left, package, psi_two)

    total = summed(mine, theirs, (turned,))
    first_rows, site, mine, theirs, *applied = call(
        second_start,
        [smem, vmem, tuple(vmem for _ in total), *[vmem] * 4],
        [rows, shape(states, states), *halves, block],
        cost=apply_cost,
    )(kept, vector, total, turned, edge, incoming, right)
    vector = second_vector
    for step in range(ITERS - 1):
        total = summed(mine, theirs)
        vector, mine, theirs, *applied = step_call(
            second_step, (vector, *applied), total, (site, edge, incoming, right), step
        )
    total = summed(mine, theirs, gathered=True)
    (second_rows,) = call(second_end, [smem, vmem, tuple(vmem for _ in total)], [rows], ())(
        kept, vector, total
    )
    return first_rows, second_rows


def solution(mesh):
    placed = (
        P("seg", "sec", None, None),
        P("seg", "sec", None, None),
        P("seg", None, None),
        P("seg", None, None),
        P("seg", None, None),
        P("seg", "sec"),
        P("seg", None),
    )
    return jax.shard_map(
        on_device,
        mesh=mesh,
        in_specs=placed,
        out_specs=(P("seg", "sec", None), P("seg", "sec", None)),
        check_vma=False,
    )
```

```python
import functools

import jax
import jax.numpy as jnp
from jax import lax
from jax.experimental import pallas as pl
from jax.experimental.pallas import tpu as pltpu
from jax.sharding import PartitionSpec as P

ITERS = 3
EPSILON = 1e-06
DESCENT = 0.3
CHUNK = 5
MIB = 1024 * 1024
GATHERED = True

F32 = jnp.float32
BF16 = jnp.bfloat16


def dot(a, b, dims=((1,), (0,))):
    return lax.dot_general(a, b, (dims, ((), ())), preferred_element_type=F32)


def live_rows(shape, live):
    return lax.broadcasted_iota(jnp.int32, shape, 0) < live


def begun(start, live):
    states = start.shape[-1]
    block = start[...].reshape(states, states).astype(F32)
    block = jnp.where(live_rows(block.shape, live), block, 0.0)
    return block * (states / jnp.sqrt(jnp.sum(block * block) + EPSILON))


def joined(summed, live):
    if len(summed) == 1:
        states = summed[0].shape[2]
        product = summed[0][...].reshape(states, states).astype(F32)
    else:
        low = lax.rem(lax.axis_index("sec"), 2) == 0
        own, far = summed[0][...].astype(F32), summed[1][...].astype(F32)
        product = jnp.concatenate([jnp.where(low, own, far), jnp.where(low, far, own)], axis=0)
    return jnp.where(live_rows(product.shape, live), product, 0.0)


def coefficients(current, product):
    states = current.shape[0]
    xx, xy = jnp.sum(current * current), jnp.sum(current * product)
    yy = jnp.sum(product * product)
    energy = xy / xx
    norm = xx + DESCENT * DESCENT * jnp.maximum(yy - energy * xy, 0.0)
    scale = states / jnp.sqrt(norm + EPSILON)
    return scale * (1.0 + DESCENT * energy), -DESCENT * scale


def stepped(vector, summed, live):
    current, product = vector[...], joined(summed, live)
    a, b = coefficients(current, product)
    return a * current + b * product


def own_rows(block, rows):
    share = rows.shape[1]
    rows[0] = block[pl.ds(pl.multiple_of(lax.axis_index("sec") * share, share), share), :]


def contract(vector, left, right, acc):
    states = vector.shape[0]
    terms = left.shape[0]
    chunk = CHUNK if terms % CHUNK == 0 else 1
    for first in range(0, terms, chunk):
        inner = dot(left[first : first + chunk].reshape(chunk * states, states), vector)
        inner = inner.astype(BF16)
        inner = [inner[n * states : (n + 1) * states] for n in range(chunk)]
        outer = right[first : first + chunk].reshape(chunk * states, states)
        total = dot(jnp.concatenate(inner, axis=1), outer)
        if first == 0:
            acc[...] = total
        else:
            acc[...] += total


def hand_out(acc, mine, theirs):
    half = mine.shape[0]
    core = lax.rem(lax.axis_index("sec"), 2)
    mine[...] = acc[pl.ds(pl.multiple_of(core * half, half), half), :].astype(BF16)
    theirs[...] = acc[pl.ds(pl.multiple_of((1 - core) * half, half), half), :].astype(BF16)


def first_start(kept, start, left, right, vector, mine, theirs, applied, acc):
    states = start.shape[2]
    block = jnp.where(live_rows((states, states), kept[0, 0]), start[0].astype(F32), 0.0)
    scale = states / jnp.sqrt(jnp.sum(block * block) + EPSILON)
    vector[...] = block * scale
    contract(block.astype(BF16), left.at[0], right.at[0], acc)
    applied[...] = acc[...] * scale
    hand_out(applied, mine, theirs)


def first_step(
    kept, vector, applied, summed, left, right, after, mine, theirs, applied_after, acc
):
    current, product = vector[...], joined(summed, kept[0, 0])
    a, b = coefficients(current, product)
    contract(product.astype(BF16), left.at[0], right.at[0], acc)
    after[...] = a * current + b * product
    applied_after[...] = a * applied[...] + b * acc[...]
    hand_out(applied_after, mine, theirs)


def place(shape):
    return lax.broadcasted_iota(jnp.int32, shape, 0), lax.broadcasted_iota(jnp.int32, shape, 1)


def wake(ready):
    ready[...] = jnp.zeros_like(ready)


def pack(gain, left, edge, ready, package):
    terms, states = left.shape[1], left.shape[2]
    row, column = place((states, states))
    pairs = terms // 2

    def scaled(n):
        return left[0, n].astype(F32) * gain[0, n]

    for n in range(pairs):
        second = scaled(2 * n + 1)
        slab = jnp.where(row >= column, scaled(2 * n), second)
        package[n * states : (n + 1) * states] = slab.astype(BF16)
        diagonal = jnp.sum(jnp.where(row == column, second, 0.0), axis=0, keepdims=True)
        base = (pairs + terms % 2 + 1) * states + 16 * n
        package[base : base + 16] = jnp.broadcast_to(diagonal, (16, states)).astype(BF16)
    if terms % 2:
        package[pairs * states : (pairs + 1) * states] = scaled(terms - 1).astype(BF16)
    last = pairs + terms % 2
    package[last * states : (last + 1) * states] = edge[0]


def unpack(kept, gain, left, package, start, incoming, site, vector, turned):
    terms, states = left.shape[1], left.shape[2]
    row, column = place((states, states))
    pairs = terms // 2
    at_start = lax.axis_index("seg") == 0

    @pl.when(at_start)
    def _():
        for n in range(terms):
            incoming[n] = (left[0, n].astype(F32) * gain[0, n]).astype(BF16)
        site[...] = jnp.where(row == column, 1.0, 0.0).astype(BF16)

    @pl.when(jnp.logical_not(at_start))
    def _():
        for n in range(pairs):
            slab = package[n * states : (n + 1) * states].astype(F32)
            mirrored = slab.T
            base = (pairs + terms % 2 + 1) * states + 16 * n
            diagonal = package[base : base + 16].astype(F32)[0:1]
            one = jnp.where(row >= column, slab, mirrored)
            two = jnp.where(row < column, slab, jnp.where(row == column, diagonal, mirrored))
            incoming[2 * n] = (one * gain[0, 2 * n]).astype(BF16)
            incoming[2 * n + 1] = (two * gain[0, 2 * n + 1]).astype(BF16)
        if terms % 2:
            slab = package[pairs * states : (pairs + 1) * states].astype(F32)
            incoming[terms - 1] = (slab * gain[0, terms - 1]).astype(BF16)
        last = pairs + terms % 2
        site[...] = package[last * states : (last + 1) * states]

    current = begun(start, kept[0, 1])
    vector[...] = current
    turned[...] = dot(site[...], current.astype(BF16)).astype(BF16)


def second_apply(inner, edge, site, incoming, right, acc):
    contract(inner, incoming, right.at[0], acc)
    outer = dot(acc[...].astype(BF16), site, ((1,), (1,))).astype(BF16)
    return dot(edge[...], outer, ((0,), (0,)))


def second_start(
    kept, vector, summed, turned, edge, incoming, right, rows, site, mine, theirs, applied, acc
):
    states = vector.shape[1]
    acc[...] = stepped(vector, summed, kept[0, 0])
    own_rows(acc, rows)
    site_left = (acc[...] * states**-0.5).astype(BF16)
    site[...] = site_left
    inner = dot(turned[...], site_left).astype(BF16)
    applied[...] = second_apply(inner, edge, site_left, incoming, right, acc)
    hand_out(applied, mine, theirs)


def second_step(
    kept, vector, applied, summed, site, edge, incoming, right,
    after, mine, theirs, applied_after, acc,
):
    current, product = vector[...], joined(summed, kept[0, 1])
    a, b = coefficients(current, product)
    inner = dot(product.astype(BF16), site[...]).astype(BF16)
    inner = dot(edge[...], inner).astype(BF16)
    found = second_apply(inner, edge, site[...], incoming, right, acc)
    after[...] = a * current + b * product
    applied_after[...] = a * applied[...] + b * found
    hand_out(applied_after, mine, theirs)


def second_end(kept, vector, summed, rows):
    live, share, half = kept[0, 1], rows.shape[1], summed[0].shape[1]
    a, b = coefficients(vector[...], joined(summed, live))
    start = lax.axis_index("sec") * share
    part = pl.ds(pl.multiple_of(lax.rem(start, half), share), share)
    product = summed[0][lax.div(start, half), part, :].astype(F32)
    product = jnp.where(live_rows(product.shape, live - start), product, 0.0)
    rows[0] = a * vector[pl.ds(pl.multiple_of(start, share), share), :] + b * product


def add(count, *refs):
    total = refs[0][...].astype(F32)
    for ref in refs[1:count]:
        total = total + ref[...].astype(F32)
    refs[-1][...] = total.astype(BF16)


def on_device(left_env, right_env, edge_site, psi_one, psi_two, mpo_gain, kept):
    terms, states = left_env.shape[1], left_env.shape[2]
    sections, segments = lax.axis_size("sec"), lax.axis_size("seg")
    share, half = states // sections, states // 2

    smem = pl.BlockSpec(memory_space=pltpu.SMEM)
    vmem = pl.BlockSpec(memory_space=pltpu.VMEM)

    def shape(*dims, dtype=BF16):
        return jax.ShapeDtypeStruct(dims, dtype)

    block = shape(states, states, dtype=F32)
    halves = [shape(half, states)] * 2
    rows = shape(1, share, states, dtype=F32)
    acc = pltpu.VMEM((states, states), F32)
    apply_cost = pl.CostEstimate(
        flops=4 * terms * states**3, bytes_accessed=4 * terms * states**2, transcendentals=0
    )

    def call(kernel, ins, outs, scratch=(acc,), limit=12 * MIB, cost=None, name=None):
        return pl.pallas_call(
            kernel,
            in_specs=ins,
            out_specs=[vmem] * len(outs),
            out_shape=outs,
            scratch_shapes=list(scratch),
            compiler_params=pltpu.CompilerParams(vmem_limit_bytes=limit),
            cost_estimate=cost,
            name=name or kernel.__name__,
        )

    def step_call(kernel, before, total, after, step):
        outs, scratch = [block, *halves], [acc]
        if step < ITERS - 2:
            outs.append(block)
        else:
            scratch.insert(0, acc)
        specs = [smem, *[vmem] * len(before), tuple(vmem for _ in total), *[vmem] * len(after)]
        return call(kernel, specs, outs, scratch, cost=apply_cost)(kept, *before, total, *after)

    def moved(value, target):
        return lax.ppermute(value, "sec", [(n, target(n) % sections) for n in range(sections)])

    def added(*values, after=()):
        kernel = functools.partial(add, len(values))
        specs = [vmem] * (len(values) + len(after))
        return call(kernel, specs, halves[:1], (), 2 * MIB, name="add")(*values, *after)[0]

    def between(chip):
        count = sections // 2
        return lambda n: 2 * (chip(n // 2, 1 if n // 2 % 2 else -1) % count) + n % 2

    cores = [[n, n + 1] for n in range(0, sections, 2)]
    near = [between(lambda z, up, far=far: z + up * far) for far in (2, 1, 3)]

    def summed(mine, theirs, after=(), gathered=GATHERED):
        total = added(mine, moved(theirs, lambda n: n ^ 1))
        total = added(total, moved(total, lambda n: n ^ 2))
        parts = [moved(total, target) for target in near]
        total = added(total, *parts, after=after)
        if gathered:
            return (lax.all_gather(total, "sec", axis=0, axis_index_groups=cores),)
        return total, moved(total, lambda n: n ^ 1)

    blocks = shape(terms, states, states)
    left, right = left_env, right_env
    slabs = terms // 2 + terms % 2 + 1
    shadow = pl.CostEstimate(
        flops=60 * terms * states**3, bytes_accessed=4 * terms * states**2, transcendentals=0
    )
    (ready,) = call(wake, [], [shape(8, 128, dtype=F32)], (), MIB, shadow)()
    (package,) = call(
        pack,
        [smem, vmem, vmem, vmem],
        [shape(slabs * states + 16 * (terms // 2), states)],
        (),
        cost=shadow,
    )(mpo_gain, left_env, edge_site, ready)
    package = lax.ppermute(package, "seg", [(n, n + 1) for n in range(segments - 1)])

    vector, mine, theirs, *applied = call(
        first_start, [smem, *[vmem] * 3], [block, *halves, block], cost=apply_cost
    )(kept, psi_one, left, right)

    for step in range(ITERS - 1):
        total = summed(mine, theirs)
        vector, mine, theirs, *applied = step_call(
            first_step, (vector, *applied), total, (left, right), step
        )

    incoming, edge, second_vector, turned = call(
        unpack,
        [smem, smem, vmem, vmem, vmem],
        [blocks, shape(states, states), block, shape(states, states)],
        (),
    )(kept, mpo_gain, left, package, psi_two)

    total = summed(mine, theirs, (turned,))
    first_rows, site, mine, theirs, *applied = call(
        second_start,
        [smem, vmem, tuple(vmem for _ in total), *[vmem] * 4],
        [rows, shape(states, states), *halves, block],
        cost=apply_cost,
    )(kept, vector, total, turned, edge, incoming, right)
    vector = second_vector
    for step in range(ITERS - 1):
        total = summed(mine, theirs)
        vector, mine, theirs, *applied = step_call(
            second_step, (vector, *applied), total, (site, edge, incoming, right), step
        )
    total = summed(mine, theirs, gathered=True)
    (second_rows,) = call(second_end, [smem, vmem, tuple(vmem for _ in total)], [rows], ())(
        kept, vector, total
    )
    return first_rows, second_rows


def solution(mesh):
    placed = (
        P("seg", "sec", None, None),
        P("seg", "sec", None, None),
        P("seg", None, None),
        P("seg", None, None),
        P("seg", None, None),
        P("seg", "sec"),
        P("seg", None),
    )
    return jax.shard_map(
        on_device,
        mesh=mesh,
        in_specs=placed,
        out_specs=(P("seg", "sec", None), P("seg", "sec", None)),
        check_vma=False,
    )
```

```python
import functools

import jax
import jax.numpy as jnp
from jax import lax
from jax.experimental import pallas as pl
from jax.experimental.pallas import tpu as pltpu
from jax.sharding import PartitionSpec as P

ITERS = 3
EPSILON = 1e-06
DESCENT = 0.3
CHUNK = 5
MIB = 1024 * 1024
GATHERED = True

F32 = jnp.float32
BF16 = jnp.bfloat16


def dot(a, b, dims=((1,), (0,))):
    return lax.dot_general(a, b, (dims, ((), ())), preferred_element_type=F32)


def live_rows(shape, live):
    return lax.broadcasted_iota(jnp.int32, shape, 0) < live


def begun(start, live):
    states = start.shape[-1]
    block = start[...].reshape(states, states).astype(F32)
    block = jnp.where(live_rows(block.shape, live), block, 0.0)
    return block * (states / jnp.sqrt(jnp.sum(block * block) + EPSILON))


def joined(summed, live):
    if len(summed) == 1:
        states = summed[0].shape[2]
        product = summed[0][...].reshape(states, states).astype(F32)
    else:
        low = lax.rem(lax.axis_index("sec"), 2) == 0
        own, far = summed[0][...].astype(F32), summed[1][...].astype(F32)
        product = jnp.concatenate([jnp.where(low, own, far), jnp.where(low, far, own)], axis=0)
    return jnp.where(live_rows(product.shape, live), product, 0.0)


def coefficients(current, product):
    states = current.shape[0]
    xx, xy = jnp.sum(current * current), jnp.sum(current * product)
    yy = jnp.sum(product * product)
    energy = xy / xx
    norm = xx + DESCENT * DESCENT * jnp.maximum(yy - energy * xy, 0.0)
    scale = states / jnp.sqrt(norm + EPSILON)
    return scale * (1.0 + DESCENT * energy), -DESCENT * scale


def stepped(vector, summed, live):
    current, product = vector[...], joined(summed, live)
    a, b = coefficients(current, product)
    return a * current + b * product


def own_rows(block, rows):
    share = rows.shape[1]
    rows[0] = block[pl.ds(pl.multiple_of(lax.axis_index("sec") * share, share), share), :]


def contract(vector, left, right, acc):
    states = vector.shape[0]
    terms = left.shape[0]
    chunk = CHUNK if terms % CHUNK == 0 else 1
    for first in range(0, terms, chunk):
        inner = dot(left[first : first + chunk].reshape(chunk * states, states), vector)
        inner = inner.astype(BF16)
        inner = [inner[n * states : (n + 1) * states] for n in range(chunk)]
        outer = right[first : first + chunk].reshape(chunk * states, states)
        total = dot(jnp.concatenate(inner, axis=1), outer)
        if first == 0:
            acc[...] = total
        else:
            acc[...] += total


def hand_out(found, mine, theirs):
    half = mine.shape[0]
    low = lax.rem(lax.axis_index("sec"), 2) == 0
    upper, lower = found[:half], found[half:]
    mine[...] = jnp.where(low, upper, lower).astype(BF16)
    theirs[...] = jnp.where(low, lower, upper).astype(BF16)


def first_start(kept, start, left, right, vector, mine, theirs, applied, acc):
    states = start.shape[2]
    block = jnp.where(live_rows((states, states), kept[0, 0]), start[0].astype(F32), 0.0)
    scale = states / jnp.sqrt(jnp.sum(block * block) + EPSILON)
    vector[...] = block * scale
    contract(block.astype(BF16), left.at[0], right.at[0], acc)
    found = acc[...] * scale
    applied[...] = found
    hand_out(found, mine, theirs)


def first_step(
    kept, vector, applied, summed, left, right, after, mine, theirs, applied_after, acc
):
    current, product = vector[...], joined(summed, kept[0, 0])
    a, b = coefficients(current, product)
    contract(product.astype(BF16), left.at[0], right.at[0], acc)
    after[...] = a * current + b * product
    found = a * applied[...] + b * acc[...]
    applied_after[...] = found
    hand_out(found, mine, theirs)


def place(shape):
    return lax.broadcasted_iota(jnp.int32, shape, 0), lax.broadcasted_iota(jnp.int32, shape, 1)


def wake(ready):
    ready[...] = jnp.zeros_like(ready)


def pack(gain, left, edge, ready, package):
    terms, states = left.shape[1], left.shape[2]
    row, column = place((states, states))
    pairs = terms // 2

    def scaled(n):
        return left[0, n].astype(F32) * gain[0, n]

    for n in range(pairs):
        second = scaled(2 * n + 1)
        slab = jnp.where(row >= column, scaled(2 * n), second)
        package[n * states : (n + 1) * states] = slab.astype(BF16)
        diagonal = jnp.sum(jnp.where(row == column, second, 0.0), axis=0, keepdims=True)
        base = (pairs + terms % 2 + 1) * states + 16 * n
        package[base : base + 16] = jnp.broadcast_to(diagonal, (16, states)).astype(BF16)
    if terms % 2:
        package[pairs * states : (pairs + 1) * states] = scaled(terms - 1).astype(BF16)
    last = pairs + terms % 2
    package[last * states : (last + 1) * states] = edge[0]


def unpack(kept, gain, left, package, start, incoming, site, vector, turned):
    terms, states = left.shape[1], left.shape[2]
    row, column = place((states, states))
    pairs = terms // 2
    at_start = lax.axis_index("seg") == 0

    @pl.when(at_start)
    def _():
        for n in range(terms):
            incoming[n] = (left[0, n].astype(F32) * gain[0, n]).astype(BF16)
        site[...] = jnp.where(row == column, 1.0, 0.0).astype(BF16)

    @pl.when(jnp.logical_not(at_start))
    def _():
        for n in range(pairs):
            slab = package[n * states : (n + 1) * states].astype(F32)
            mirrored = slab.T
            base = (pairs + terms % 2 + 1) * states + 16 * n
            diagonal = package[base : base + 16].astype(F32)[0:1]
            one = jnp.where(row >= column, slab, mirrored)
            two = jnp.where(row < column, slab, jnp.where(row == column, diagonal, mirrored))
            incoming[2 * n] = (one * gain[0, 2 * n]).astype(BF16)
            incoming[2 * n + 1] = (two * gain[0, 2 * n + 1]).astype(BF16)
        if terms % 2:
            slab = package[pairs * states : (pairs + 1) * states].astype(F32)
            incoming[terms - 1] = (slab * gain[0, terms - 1]).astype(BF16)
        last = pairs + terms % 2
        site[...] = package[last * states : (last + 1) * states]

    current = begun(start, kept[0, 1])
    vector[...] = current
    turned[...] = dot(site[...], current.astype(BF16)).astype(BF16)


def second_apply(inner, edge, site, incoming, right, acc):
    contract(inner, incoming, right.at[0], acc)
    outer = dot(acc[...].astype(BF16), site, ((1,), (1,))).astype(BF16)
    return dot(edge[...], outer, ((0,), (0,)))


def second_start(
    kept, vector, summed, turned, edge, incoming, right, rows, site, mine, theirs, applied, acc
):
    states = vector.shape[1]
    current, product = vector[...], joined(summed, kept[0, 0])
    a, b = coefficients(current, product)
    old, new = dot(turned[...], current.astype(BF16)), dot(turned[...], product.astype(BF16))
    acc[...] = a * current + b * product
    own_rows(acc, rows)
    site_left = (acc[...] * states**-0.5).astype(BF16)
    site[...] = site_left
    inner = ((a * states**-0.5) * old + (b * states**-0.5) * new).astype(BF16)
    found = second_apply(inner, edge, site_left, incoming, right, acc)
    applied[...] = found
    hand_out(found, mine, theirs)


def second_step(
    kept, vector, applied, summed, site, edge, incoming, right,
    after, mine, theirs, applied_after, acc,
):
    current, product = vector[...], joined(summed, kept[0, 1])
    a, b = coefficients(current, product)
    inner = dot(product.astype(BF16), site[...]).astype(BF16)
    inner = dot(edge[...], inner).astype(BF16)
    found = second_apply(inner, edge, site[...], incoming, right, acc)
    after[...] = a * current + b * product
    found = a * applied[...] + b * found
    applied_after[...] = found
    hand_out(found, mine, theirs)


def second_end(kept, vector, summed, rows):
    live, share, half = kept[0, 1], rows.shape[1], summed[0].shape[1]
    a, b = coefficients(vector[...], joined(summed, live))
    start = lax.axis_index("sec") * share
    part = pl.ds(pl.multiple_of(lax.rem(start, half), share), share)
    product = summed[0][lax.div(start, half), part, :].astype(F32)
    product = jnp.where(live_rows(product.shape, live - start), product, 0.0)
    rows[0] = a * vector[pl.ds(pl.multiple_of(start, share), share), :] + b * product


def add(count, *refs):
    total = refs[0][...].astype(F32)
    for ref in refs[1:count]:
        total = total + ref[...].astype(F32)
    refs[-1][...] = total.astype(BF16)


def on_device(left_env, right_env, edge_site, psi_one, psi_two, mpo_gain, kept):
    terms, states = left_env.shape[1], left_env.shape[2]
    sections, segments = lax.axis_size("sec"), lax.axis_size("seg")
    share, half = states // sections, states // 2

    smem = pl.BlockSpec(memory_space=pltpu.SMEM)
    vmem = pl.BlockSpec(memory_space=pltpu.VMEM)

    def shape(*dims, dtype=BF16):
        return jax.ShapeDtypeStruct(dims, dtype)

    block = shape(states, states, dtype=F32)
    halves = [shape(half, states)] * 2
    rows = shape(1, share, states, dtype=F32)
    acc = pltpu.VMEM((states, states), F32)
    apply_cost = pl.CostEstimate(
        flops=4 * terms * states**3, bytes_accessed=4 * terms * states**2, transcendentals=0
    )

    def call(kernel, ins, outs, scratch=(acc,), limit=12 * MIB, cost=None, name=None):
        return pl.pallas_call(
            kernel,
            in_specs=ins,
            out_specs=[vmem] * len(outs),
            out_shape=outs,
            scratch_shapes=list(scratch),
            compiler_params=pltpu.CompilerParams(vmem_limit_bytes=limit),
            cost_estimate=cost,
            name=name or kernel.__name__,
        )

    def step_call(kernel, before, total, after, step):
        outs, scratch = [block, *halves], [acc]
        if step < ITERS - 2:
            outs.append(block)
        else:
            scratch.insert(0, acc)
        specs = [smem, *[vmem] * len(before), tuple(vmem for _ in total), *[vmem] * len(after)]
        return call(kernel, specs, outs, scratch, cost=apply_cost)(kept, *before, total, *after)

    def moved(value, target):
        return lax.ppermute(value, "sec", [(n, target(n) % sections) for n in range(sections)])

    def added(*values, after=()):
        kernel = functools.partial(add, len(values))
        specs = [vmem] * (len(values) + len(after))
        return call(kernel, specs, halves[:1], (), 2 * MIB, name="add")(*values, *after)[0]

    def between(chip):
        count = sections // 2
        return lambda n: 2 * (chip(n // 2, 1 if n // 2 % 2 else -1) % count) + n % 2

    cores = [[n, n + 1] for n in range(0, sections, 2)]
    near = [between(lambda z, up, far=far: z + up * far) for far in (2, 1, 3)]

    def summed(mine, theirs, after=(), gathered=GATHERED):
        total = added(mine, moved(theirs, lambda n: n ^ 1))
        total = added(total, moved(total, lambda n: n ^ 2))
        parts = [moved(total, target) for target in near]
        total = added(total, *parts, after=after)
        if gathered:
            return (lax.all_gather(total, "sec", axis=0, axis_index_groups=cores),)
        return total, moved(total, lambda n: n ^ 1)

    blocks = shape(terms, states, states)
    left, right = left_env, right_env
    slabs = terms // 2 + terms % 2 + 1
    shadow = pl.CostEstimate(
        flops=60 * terms * states**3, bytes_accessed=4 * terms * states**2, transcendentals=0
    )
    (ready,) = call(wake, [], [shape(8, 128, dtype=F32)], (), MIB, shadow)()
    (package,) = call(
        pack,
        [smem, vmem, vmem, vmem],
        [shape(slabs * states + 16 * (terms // 2), states)],
        (),
        cost=shadow,
    )(mpo_gain, left_env, edge_site, ready)
    package = lax.ppermute(package, "seg", [(n, n + 1) for n in range(segments - 1)])

    vector, mine, theirs, *applied = call(
        first_start, [smem, *[vmem] * 3], [block, *halves, block], cost=apply_cost
    )(kept, psi_one, left, right)

    for step in range(ITERS - 1):
        total = summed(mine, theirs)
        vector, mine, theirs, *applied = step_call(
            first_step, (vector, *applied), total, (left, right), step
        )

    incoming, edge, second_vector, turned = call(
        unpack,
        [smem, smem, vmem, vmem, vmem],
        [blocks, shape(states, states), block, shape(states, states)],
        (),
    )(kept, mpo_gain, left, package, psi_two)

    total = summed(mine, theirs, (turned,))
    first_rows, site, mine, theirs, *applied = call(
        second_start,
        [smem, vmem, tuple(vmem for _ in total), *[vmem] * 4],
        [rows, shape(states, states), *halves, block],
        cost=apply_cost,
    )(kept, vector, total, turned, edge, incoming, right)
    vector = second_vector
    for step in range(ITERS - 1):
        total = summed(mine, theirs)
        vector, mine, theirs, *applied = step_call(
            second_step, (vector, *applied), total, (site, edge, incoming, right), step
        )
    total = summed(mine, theirs, gathered=True)
    (second_rows,) = call(second_end, [smem, vmem, tuple(vmem for _ in total)], [rows], ())(
        kept, vector, total
    )
    return first_rows, second_rows


def solution(mesh):
    placed = (
        P("seg", "sec", None, None),
        P("seg", "sec", None, None),
        P("seg", None, None),
        P("seg", None, None),
        P("seg", None, None),
        P("seg", "sec"),
        P("seg", None),
    )
    return jax.shard_map(
        on_device,
        mesh=mesh,
        in_specs=placed,
        out_specs=(P("seg", "sec", None), P("seg", "sec", None)),
        check_vma=False,
    )
```
